128 devices in a mesh: fsdp: 8 (over x, core), tp: 16 (over y, z).
Axes of the slice: x: 4, y: 4, z: 4, core: 2. Of those that a mesh axis runs over, the one named last changes fastest.
Arguments:
- grad: bfloat16 [3072, 16384], P('fsdp', 'tp'), may hold values from -0.375 to 0.375
- left_stat: float32 [128, 1024, 1024], P(('fsdp', 'tp')), as said below
- right_stat: float32 [128, 1024, 1024], P(('fsdp', 'tp')), as said below
- left_root: bfloat16 [128, 1024, 1024], P(('fsdp', 'tp')), as said below
- right_root: bfloat16 [128, 1024, 1024], P(('fsdp', 'tp')), as said below
- block_owner: int32 [48], replicated, may hold values from 0 to 127, as said below
- owner_block: int32 [128], replicated, may hold values from 0 to 47, as said below
- owner_count: int32 [128], replicated, may hold values from 0 to 1, as said below
Outputs:
- new_left: float32 [128, 1024, 1024], P(('fsdp', 'tp'))
- new_right: float32 [128, 1024, 1024], P(('fsdp', 'tp'))
- update: bfloat16 [3072, 16384], P('fsdp', 'tp')
The draws below stay inside these ranges and needn't reach their ends.
Inputs may be any that keep to these rules, and one draw needn't show every extreme that they name: `block_owner`: the entries are distinct. Owner o is the device with fsdp index o // 16 and tp index o % 16. `owner_block`: for an owner with count 1, the block b with block_owner[b] equal to that owner; 0 for an owner with count 0. `owner_count`: 1 exactly for the owners named in block_owner. `left_stat`: Symmetric. `right_stat`: Symmetric. `left_root`: Symmetric. `right_root`: Symmetric.
All inputs are finite; a program needn't handle non-finite values.
Results may differ from the reference program's by a relative error of at most 0.0049.
Values may be sent and summed in bfloat16 or wider, within the bound.
A program may use at most 64 MiB of HBM per device.

```python
import jax
import jax.numpy as jnp
from jax import lax

D = 3072
BS = 1024
FFW = 16384
RB = 3
NB = 48
OWNERS = 128


def owner_table(key):
    shuffled = jax.random.permutation(key, OWNERS).astype(jnp.int32)
    position = jnp.argsort(shuffled).astype(jnp.int32)
    return (shuffled, position)


def assemble(noise_field, diagonal, spread):
    symmetric = (noise_field + jnp.swapaxes(noise_field, 1, 2)) * (spread / (2.0 * BS) ** 0.5)
    identity = jnp.eye(BS, dtype=jnp.float32)
    return symmetric * (1.0 - identity) + diagonal[:, :, None] * identity


def square_draw(key, low, high, spread):
    key_noise, key_diag = jax.random.split(key)
    noise_field = jax.random.normal(key_noise, (OWNERS, BS, BS), jnp.float32)
    diagonal = jax.random.uniform(key_diag, (OWNERS, BS), jnp.float32, low, high)
    return assemble(noise_field, diagonal, spread)


def draw_block_owner(key, part):
    shuffled, position = owner_table(key)
    return shuffled[:NB]


def draw_owner_block(key, part):
    shuffled, position = owner_table(key)
    return jnp.where(position < NB, position, 0).astype(jnp.int32)


def draw_owner_count(key, part):
    shuffled, position = owner_table(key)
    return (position < NB).astype(jnp.int32)


def draw_left_stat(key, part):
    key = jax.random.fold_in(key, 11)
    return square_draw(key, 2.0, 8.0, 1.5)


def draw_right_stat(key, part):
    key = jax.random.fold_in(key, 12)
    return square_draw(key, 2.0, 8.0, 1.5)


def draw_left_root(key, part):
    key = jax.random.fold_in(key, 13)
    return square_draw(key, 2.0, 4.0, 0.8).astype(jnp.bfloat16)


def draw_right_root(key, part):
    key = jax.random.fold_in(key, 14)
    return square_draw(key, 2.0, 4.0, 0.8).astype(jnp.bfloat16)


def levels(rng, extent, shards, smallest, largest):
    def one(dim, shards_of):
        draws = jax.random.uniform(jax.random.fold_in(jax.random.fold_in(rng, 6), dim), (shards_of,), jnp.float32, smallest / len(shards), largest / len(shards))
        return jnp.repeat(jnp.exp(draws), extent[dim] // shards_of).reshape((-1,) + (1,) * (len(extent) - dim - 1))

    loudness = one(*shards[0])
    for cut in shards[1:]:
        loudness = loudness * one(*cut)
    return loudness


def centred(own_key, dims, scale, most, cuts=(), kind=jnp.bfloat16):
    entries = scale * jax.random.normal(own_key, dims, jnp.float32)
    if cuts:
        entries = entries * levels(own_key, dims, cuts, -0.22, 0.18)
    return jnp.clip(entries, -most, most).astype(kind)


def setup_inputs(seed: int = 0) -> dict:
    seeds = jax.random.split(jax.random.key(seed), 9)
    return {
        "grad": centred(seeds[0], (D, FFW), (BS // 4) ** -0.5, 0.375, ((0, 8), (1, 16))),
        "left_stat": draw_left_stat(jax.random.fold_in(seeds[8], 71), 0),
        "right_stat": draw_right_stat(jax.random.fold_in(seeds[8], 71), 0),
        "left_root": draw_left_root(jax.random.fold_in(seeds[8], 71), 0),
        "right_root": draw_right_root(jax.random.fold_in(seeds[8], 71), 0),
        "block_owner": draw_block_owner(jax.random.fold_in(seeds[8], 71), 0),
        "owner_block": draw_owner_block(jax.random.fold_in(seeds[8], 71), 0),
        "owner_count": draw_owner_count(jax.random.fold_in(seeds[8], 71), 0),
    }


def reference(grad, left_stat, right_stat, left_root, right_root, block_owner, owner_block, owner_count):
    grid_blocks = grad.reshape(RB, BS, FFW // BS, BS).transpose(0, 2, 1, 3).reshape(NB, BS, BS)

    def stats_one(holder):
        chosen = grid_blocks[owner_block[holder]] * owner_count[holder].astype(jnp.bfloat16)
        gram_left = jnp.dot(chosen, chosen.T, preferred_element_type=jnp.float32)
        gram_right = jnp.dot(chosen.T, chosen, preferred_element_type=jnp.float32)
        return left_stat[holder] + gram_left, right_stat[holder] + gram_right

    new_left, new_right = lax.map(stats_one, jnp.arange(OWNERS, dtype=jnp.int32))

    def precondition(block_id):
        holder = block_owner[block_id]
        mixed_rows = jnp.dot(left_root[holder], grid_blocks[block_id], preferred_element_type=jnp.float32).astype(jnp.bfloat16)
        return jnp.dot(mixed_rows, right_root[holder], preferred_element_type=jnp.float32).astype(jnp.bfloat16)

    finished = lax.map(precondition, jnp.arange(NB, dtype=jnp.int32))
    update = finished.reshape(RB, FFW // BS, BS, BS).transpose(0, 2, 1, 3).reshape(D, FFW)
    return (new_left, new_right, update)
```

```python
import jax
import jax.numpy as jnp
from jax import lax
from jax.experimental import pallas as pl
from jax.experimental.pallas import tpu as pltpu
from jax.sharding import PartitionSpec as P

MESH = pl.DeviceIdType.MESH
BS = 1024
FS = 8
TP = 16
NB = 48
OWNERS = FS * TP
CHUNK = BS // FS
RR, RC = 16, 512
PER = 3


def region_rows(chunk, t):
    return pl.ds(pl.multiple_of(chunk * CHUNK + (t // 2) * RR, RR), RR)


def region_cols(t):
    return pl.ds(pl.multiple_of((t % 2) * RC, RC), RC)


def swapped(k):
    return (k // 4) * 4 + 3 - k % 4


def shifted_t(t, n):
    return ((t // 4 + n // 4) % 4) * 4 + (t % 4 + n % 4) % 4


def shifted_f(f, n):
    return ((f // 2 + n // 2) % 4) * 2 + (f % 2 + n % 2) % 2


def wait_bytes(ref, sem):
    pltpu.make_async_copy(ref, ref, sem).wait()


def route_kernel(
    owner_block, block_owner, grad, left_root, right_root,
    held, update,
    inter, stage, mixed, done, ret, back,
    send_sem, recv_sem,
):
    f = lax.axis_index("fsdp")
    t = lax.axis_index("tp")
    me = f * TP + t
    my_chunk = swapped(f)

    barrier = pltpu.get_barrier_semaphore()

    @pl.loop(1, OWNERS)
    def _(n):
        o = (me + n) % OWNERS
        pl.semaphore_signal(barrier, inc=1, device_id=(o // TP, o % TP), device_id_type=MESH)

    pl.semaphore_wait(barrier, OWNERS - 1)

    @pl.loop(0, PER * TP)
    def _(n):
        q = n % PER
        chunk = f * PER + q
        to_t = shifted_t(t, n // PER)
        pltpu.make_async_remote_copy(
            src_ref=grad.at[region_rows(q, to_t), region_cols(to_t)],
            dst_ref=inter.at[(chunk // FS) * TP + t],
            send_sem=send_sem.at[0],
            recv_sem=recv_sem.at[0],
            device_id=(swapped(chunk % FS), to_t),
            device_id_type=MESH,
        ).start()

    wait_bytes(inter, recv_sem.at[0])

    stage[me] = inter[owner_block[me]]
    pltpu.make_async_copy(
        stage.at[me], held.at[region_rows(my_chunk, t), region_cols(t)], recv_sem.at[1]
    ).start()

    @pl.loop(1, OWNERS)
    def _(n):
        m = (n * 37) % OWNERS
        to_f = shifted_f(f, m // TP)
        to_t = shifted_t(t, m % TP)
        o = to_f * TP + to_t
        stage[o] = inter[owner_block[o]]
        pltpu.make_async_remote_copy(
            src_ref=stage.at[o],
            dst_ref=held.at[region_rows(my_chunk, t), region_cols(t)],
            send_sem=send_sem.at[1],
            recv_sem=recv_sem.at[1],
            device_id=(to_f, to_t),
            device_id_type=MESH,
        ).start()

    wait_bytes(held, recv_sem.at[1])

    @pl.loop(0, 4)
    def _(c):
        rows = pl.ds(pl.multiple_of(c * 256, 256), 256)
        mixed[rows, :] = jnp.dot(
            left_root[rows, :], held[...], preferred_element_type=jnp.float32
        ).astype(jnp.bfloat16)

    @pl.loop(0, 4)
    def _(c):
        rows = pl.ds(pl.multiple_of(c * 256, 256), 256)
        done[rows, :] = jnp.dot(
            mixed[rows, :], right_root[...], preferred_element_type=jnp.float32
        ).astype(jnp.bfloat16)

    pltpu.make_async_copy(
        done.at[region_rows(my_chunk, t), region_cols(t)], ret.at[me], recv_sem.at[2]
    ).start()

    @pl.loop(1, OWNERS)
    def _(n):
        m = (n * 37) % OWNERS
        to_f = shifted_f(f, m // TP)
        to_t = shifted_t(t, m % TP)
        pltpu.make_async_remote_copy(
            src_ref=done.at[region_rows(swapped(to_f), to_t), region_cols(to_t)],
            dst_ref=ret.at[me],
            send_sem=send_sem.at[2],
            recv_sem=recv_sem.at[2],
            device_id=(to_f, to_t),
            device_id_type=MESH,
        ).start()

    wait_bytes(ret, recv_sem.at[2])

    @pl.loop(0, NB)
    def _(n):
        band = n % PER
        to_t = shifted_t(t, n // PER)
        b = band * TP + to_t
        chunk = band * FS + my_chunk
        back[b] = ret[block_owner[b]]
        pltpu.make_async_remote_copy(
            src_ref=back.at[b],
            dst_ref=update.at[region_rows(chunk % PER, t), region_cols(t)],
            send_sem=send_sem.at[3],
            recv_sem=recv_sem.at[3],
            device_id=(chunk // PER, to_t),
            device_id_type=MESH,
        ).start()

    wait_bytes(inter, send_sem.at[0])
    wait_bytes(stage.at[pl.ds(0, OWNERS - 1)], send_sem.at[1])
    wait_bytes(ret.at[pl.ds(0, OWNERS - 1)], send_sem.at[2])
    wait_bytes(back, send_sem.at[3])
    wait_bytes(update, recv_sem.at[3])


def route(owner_block, block_owner, grad, left_root, right_root):
    vmem = pl.BlockSpec(memory_space=pltpu.VMEM)
    smem = pl.BlockSpec(memory_space=pltpu.SMEM)
    return pl.pallas_call(
        route_kernel,
        out_shape=(
            jax.ShapeDtypeStruct((BS, BS), jnp.bfloat16),
            jax.ShapeDtypeStruct(grad.shape, jnp.bfloat16),
        ),
        in_specs=[smem, smem, vmem, vmem, vmem],
        out_specs=(vmem, vmem),
        scratch_shapes=[
            pltpu.VMEM((NB, RR, RC), jnp.bfloat16),
            pltpu.VMEM((OWNERS, RR, RC), jnp.bfloat16),
            pltpu.VMEM((BS, BS), jnp.bfloat16),
            pltpu.VMEM((BS, BS), jnp.bfloat16),
            pltpu.VMEM((OWNERS, RR, RC), jnp.bfloat16),
            pltpu.VMEM((NB, RR, RC), jnp.bfloat16),
            pltpu.SemaphoreType.DMA((4,)),
            pltpu.SemaphoreType.DMA((4,)),
        ],
        compiler_params=pltpu.CompilerParams(
            collective_id=0, has_side_effects=True, vmem_limit_bytes=40 * 1024 * 1024
        ),
        cost_estimate=pl.CostEstimate(
            flops=4 * BS**3, bytes_accessed=12 * BS * BS, transcendentals=0
        ),
        name="route",
    )(owner_block, block_owner, grad, left_root, right_root)


def body(grad, left_stat, right_stat, left_root, right_root, block_owner, owner_block, owner_count):
    me = lax.axis_index("fsdp") * TP + lax.axis_index("tp")
    own_block, update = route(owner_block, block_owner, grad, left_root[0], right_root[0])
    held = own_block * owner_count[me].astype(jnp.bfloat16)
    gram_left = lax.dot_general(
        held, held, (((1,), (1,)), ((), ())), preferred_element_type=jnp.float32
    )
    gram_right = lax.dot_general(
        held, held, (((0,), (0,)), ((), ())), preferred_element_type=jnp.float32
    )
    return (left_stat[0] + gram_left)[None], (right_stat[0] + gram_right)[None], update


def solution(mesh):
    whole = P(("fsdp", "tp"), None, None)
    return jax.shard_map(
        body,
        mesh=mesh,
        in_specs=(P("fsdp", "tp"), whole, whole, whole, whole, P(), P(), P()),
        out_specs=(whole, whole, P("fsdp", "tp")),
        check_vma=False,
    )
```

```python
import jax
import jax.numpy as jnp
from jax import lax
from jax.experimental import pallas as pl
from jax.experimental.pallas import tpu as pltpu
from jax.sharding import PartitionSpec as P

MESH = pl.DeviceIdType.MESH
BS = 1024
HALF = BS // 2
FS = 8
TP = 16
NB = 48
OWNERS = FS * TP
CHUNK = BS // FS
RR, RC = 16, 512
PER = 3
STEP = 256


def region_rows(chunk, t):
    return pl.ds(pl.multiple_of(chunk * CHUNK + (t // 2) * RR, RR), RR)


def region_cols(t):
    return pl.ds(pl.multiple_of((t % 2) * RC, RC), RC)


def chunk_to_f(k):
    return 2 * ((2 * (k % 4) + 1) % 5) + 1 - k // 4


def f_to_chunk(f):
    return (3 * (f // 2) + 2) % 5 + 4 * (1 - f % 2)


def shifted_t(t, n):
    return ((t // 4 + n // 4) % 4) * 4 + (t % 4 + n % 4) % 4


def wait_bytes(ref, sem):
    pltpu.make_async_copy(ref, ref, sem).wait()


def steps(first, last):
    def over(fn):
        @pl.loop(first // STEP, last // STEP)
        def _(c):
            fn(pl.ds(pl.multiple_of(c * STEP, STEP), STEP))

    return over


def route_kernel(
    owner_block_any, block_owner_any, owner_count_any, grad_any,
    left_root_any, right_root_any, left_stat_any, right_stat_any,
    new_left, new_right, update,
    owner_block, block_owner, owner_count, grad, left_root, right_root,
    inter, stage, held, total, mixed, done, ret, back,
    local_sem, send_sem, recv_sem, land_sem,
):
    f = lax.axis_index("fsdp")
    t = lax.axis_index("tp")
    me = f * TP + t
    x, core = f // 2, f % 2
    my_chunk = f_to_chunk(f)

    fetches = [
        pltpu.make_async_copy(src, dst, local_sem.at[i])
        for i, (src, dst) in enumerate((
            (owner_block_any, owner_block),
            (block_owner_any, block_owner),
            (owner_count_any, owner_count),
            (grad_any, grad),
            (left_root_any, left_root),
            (right_root_any, right_root),
            (left_stat_any, new_left),
            (right_stat_any, new_right),
        ))
    ]
    for fetch in fetches:
        fetch.start()

    barrier = pltpu.get_barrier_semaphore()

    @pl.loop(1, OWNERS)
    def _(n):
        o = (me + n) % OWNERS
        pl.semaphore_signal(barrier, inc=1, device_id=(o // TP, o % TP), device_id_type=MESH)

    for fetch in fetches[:4]:
        fetch.wait()
    pl.semaphore_wait(barrier, OWNERS - 1)

    for part in range(2):
        for q in range(PER):
            chunk = f * PER + q
            k = chunk % FS

            @pl.when(k // 4 == part)
            def _():
                @pl.loop(0, TP)
                def _(n):
                    to_t = shifted_t(t, n)
                    pltpu.make_async_remote_copy(
                        src_ref=grad.at[region_rows(q, to_t), region_cols(to_t)],
                        dst_ref=inter.at[(chunk // FS) * TP + t],
                        send_sem=send_sem.at[0],
                        recv_sem=recv_sem.at[0],
                        device_id=(chunk_to_f(k), to_t),
                        device_id_type=MESH,
                    ).start()

    wait_bytes(inter, recv_sem.at[0])

    stage[me] = inter[owner_block[me]]
    pltpu.make_async_copy(
        stage.at[me], held.at[region_rows(my_chunk, t), region_cols(t)], land_sem.at[1 - core]
    ).start()

    @pl.loop(1, OWNERS)
    def _(n):
        m = (n * 37) % OWNERS
        to_f = ((x + m // 32) % 4) * 2 + (core + m // 16) % 2
        to_t = shifted_t(t, m % TP)
        o = to_f * TP + to_t
        stage[o] = inter[owner_block[o]]
        pltpu.make_async_remote_copy(
            src_ref=stage.at[o],
            dst_ref=held.at[region_rows(my_chunk, t), region_cols(t)],
            send_sem=send_sem.at[1],
            recv_sem=land_sem.at[1 - core],
            device_id=(to_f, to_t),
            device_id_type=MESH,
        ).start()

    fetches[4].wait()
    fetches[5].wait()
    wait_bytes(held.at[pl.ds(0, HALF)], land_sem.at[0])

    @steps(0, BS)
    def _(rows):
        total[rows, :] = jnp.dot(
            left_root[rows, pl.ds(0, HALF)], held[pl.ds(0, HALF), :],
            preferred_element_type=jnp.float32,
        )

    wait_bytes(held.at[pl.ds(HALF, HALF)], land_sem.at[1])

    for part in range(2):
        @steps(part * HALF, (part + 1) * HALF)
        def _(rows):
            mixed[rows, :] = (
                total[rows, :]
                + jnp.dot(
                    left_root[rows, pl.ds(HALF, HALF)], held[pl.ds(HALF, HALF), :],
                    preferred_element_type=jnp.float32,
                )
            ).astype(jnp.bfloat16)
            done[rows, :] = jnp.dot(
                mixed[rows, :], right_root[...], preferred_element_type=jnp.float32
            ).astype(jnp.bfloat16)

        to_core = 1 - part

        @pl.when(core == to_core)
        def _():
            pltpu.make_async_copy(
                done.at[region_rows(my_chunk, t), region_cols(t)], ret.at[me], recv_sem.at[1]
            ).start()

        def send_back(n):
            to_f = ((x + n // TP) % 4) * 2 + to_core
            to_t = shifted_t(t, n % TP)
            pltpu.make_async_remote_copy(
                src_ref=done.at[region_rows(f_to_chunk(to_f), to_t), region_cols(to_t)],
                dst_ref=ret.at[me],
                send_sem=send_sem.at[2],
                recv_sem=recv_sem.at[1],
                device_id=(to_f, to_t),
                device_id_type=MESH,
            ).start()

        @pl.when(core != to_core)
        def _():
            send_back(0)

        @pl.loop(1, OWNERS // 2)
        def _(n):
            send_back((n * 37) % (OWNERS // 2))

    count = owner_count[me].astype(jnp.float32)
    fetches[7].wait()

    @steps(0, BS)
    def _(rows):
        new_right[rows, :] += count * lax.dot_general(
            held[:, rows], held[...], (((0,), (0,)), ((), ())),
            preferred_element_type=jnp.float32,
        )

    wait_bytes(ret, recv_sem.at[1])

    @pl.loop(0, NB)
    def _(n):
        band = n % PER
        to_t = shifted_t(t, n // PER)
        b = band * TP + to_t
        chunk = band * FS + my_chunk
        back[b] = ret[block_owner[b]]
        pltpu.make_async_remote_copy(
            src_ref=back.at[b],
            dst_ref=update.at[region_rows(chunk % PER, t), region_cols(t)],
            send_sem=send_sem.at[3],
            recv_sem=recv_sem.at[2],
            device_id=(chunk // PER, to_t),
            device_id_type=MESH,
        ).start()

    fetches[6].wait()

    @steps(0, BS)
    def _(rows):
        new_left[rows, :] += count * lax.dot_general(
            held[rows, :], held[...], (((1,), (1,)), ((), ())),
            preferred_element_type=jnp.float32,
        )

    wait_bytes(inter, send_sem.at[0])
    wait_bytes(stage.at[pl.ds(0, OWNERS - 1)], send_sem.at[1])
    wait_bytes(ret.at[pl.ds(0, OWNERS - 1)], send_sem.at[2])
    wait_bytes(back, send_sem.at[3])
    wait_bytes(update, recv_sem.at[2])


def route(*operands):
    grad = operands[3]
    vmem = pl.BlockSpec(memory_space=pltpu.VMEM)
    stat = pltpu.VMEM((BS, BS), jnp.float32)
    square = pltpu.VMEM((BS, BS), jnp.bfloat16)
    return pl.pallas_call(
        route_kernel,
        out_shape=(stat, stat, pltpu.VMEM(grad.shape, jnp.bfloat16)),
        in_specs=[pl.BlockSpec(memory_space=pltpu.HBM)] * 8,
        out_specs=(vmem,) * 3,
        scratch_shapes=[
            pltpu.SMEM((OWNERS,), jnp.int32),
            pltpu.SMEM((NB,), jnp.int32),
            pltpu.SMEM((OWNERS,), jnp.int32),
            pltpu.VMEM(grad.shape, jnp.bfloat16),
            square,
            square,
            pltpu.VMEM((NB, RR, RC), jnp.bfloat16),
            pltpu.VMEM((OWNERS, RR, RC), jnp.bfloat16),
            square,
            pltpu.VMEM((BS, BS), jnp.float32),
            square,
            square,
            pltpu.VMEM((OWNERS, RR, RC), jnp.bfloat16),
            pltpu.VMEM((NB, RR, RC), jnp.bfloat16),
            pltpu.SemaphoreType.DMA((8,)),
            pltpu.SemaphoreType.DMA((4,)),
            pltpu.SemaphoreType.DMA((3,)),
            pltpu.SemaphoreType.DMA((2,)),
        ],
        compiler_params=pltpu.CompilerParams(
            collective_id=0, has_side_effects=True, vmem_limit_bytes=40 * 1024 * 1024
        ),
        cost_estimate=pl.CostEstimate(
            flops=8 * BS**3, bytes_accessed=24 * BS * BS, transcendentals=0
        ),
        name="route",
    )(*(pltpu.with_memory_space_constraint(a, pltpu.HBM) for a in operands))


def write_kernel(left, right, update, left_out, right_out, update_out, sems):
    copies = []
    for src, dst, parts in ((left, left_out, 4), (right, right_out, 4), (update, update_out, 1)):
        rows = src.shape[0] // parts
        for i in range(parts):
            piece = pl.ds(i * rows, rows)
            copies.append(pltpu.make_async_copy(src.at[piece], dst.at[piece], sems.at[len(copies)]))
    for copy in copies:
        copy.start()
    for copy in copies:
        copy.wait()


def write(*arrays):
    return pl.pallas_call(
        write_kernel,
        out_shape=tuple(jax.ShapeDtypeStruct(a.shape, a.dtype) for a in arrays),
        in_specs=[pl.BlockSpec(memory_space=pltpu.VMEM)] * 3,
        out_specs=(pl.BlockSpec(memory_space=pltpu.HBM),) * 3,
        scratch_shapes=[pltpu.SemaphoreType.DMA((9,))],
        compiler_params=pltpu.CompilerParams(vmem_limit_bytes=1024 * 1024),
        cost_estimate=pl.CostEstimate(flops=0, bytes_accessed=18 * BS * BS, transcendentals=0),
        name="write",
    )(*(pltpu.with_memory_space_constraint(a, pltpu.VMEM) for a in arrays))


def body(grad, left_stat, right_stat, left_root, right_root, block_owner, owner_block, owner_count):
    new_left, new_right, update = write(*route(
        owner_block, block_owner, owner_count, grad,
        left_root[0], right_root[0], left_stat[0], right_stat[0],
    ))
    return new_left[None], new_right[None], update


def solution(mesh):
    whole = P(("fsdp", "tp"), None, None)
    return jax.shard_map(
        body,
        mesh=mesh,
        in_specs=(P("fsdp", "tp"), whole, whole, whole, whole, P(), P(), P()),
        out_specs=(whole, whole, P("fsdp", "tp")),
        check_vma=False,
    )
```

```python
import jax
import jax.numpy as jnp
from jax import lax
from jax.experimental import pallas as pl
from jax.experimental.pallas import tpu as pltpu
from jax.sharding import PartitionSpec as P

MESH = pl.DeviceIdType.MESH
BS = 1024
HALF = BS // 2
FS = 8
TP = 16
NB = 48
OWNERS = FS * TP
CHUNK = BS // FS
RR, RC = 16, 256
PER = 3
STEP = 256


def piece(chunk, half, t):
    return (
        pl.ds(pl.multiple_of(chunk * CHUNK + (t // 2) * RR, RR), RR),
        pl.ds(pl.multiple_of(half * HALF + (t % 2) * RC, RC), RC),
    )


def swapped(k):
    return (k // 4) * 4 + 3 - k % 4


def shifted_t(t, n):
    return ((t // 4 + n // 4) % 4) * 4 + (t % 4 + n % 4) % 4


def wait_bytes(ref, sem):
    pltpu.make_async_copy(ref, ref, sem).wait()


def steps(first, last):
    def over(fn):
        @pl.loop(first // STEP, last // STEP)
        def _(c):
            fn(pl.ds(pl.multiple_of(c * STEP, STEP), STEP))

    return over


def route_kernel(
    owner_block_any, block_owner_any, owner_count_any, grad_any,
    left_root_any, right_root_any, left_stat_any, right_stat_any,
    new_left, new_right, update,
    owner_block, block_owner, owner_count, grad, left_root, right_root,
    inter_0, inter_1, stage, held, total, mixed, done, ret_0, ret_1, back,
    local_sem, send_sem, recv_sem, heard_sem,
):
    f = lax.axis_index("fsdp")
    t = lax.axis_index("tp")
    me = f * TP + t
    x, core = f // 2, f % 2
    my_chunk = swapped(f)
    inter, ret = (inter_0, inter_1), (ret_0, ret_1)
    halves = [pl.ds(h * HALF, HALF) for h in range(2)]

    fetches = [
        pltpu.make_async_copy(src, dst, local_sem.at[i])
        for i, (src, dst) in enumerate((
            (owner_block_any, owner_block),
            (block_owner_any, block_owner),
            (owner_count_any, owner_count),
            (grad_any, grad),
            (left_root_any, left_root),
            (right_root_any, right_root),
            (left_stat_any, new_left),
            (right_stat_any, new_right),
        ))
    ]
    for fetch in fetches[:4]:
        fetch.start()

    targets = [swapped((f * PER + q) % FS) for q in range(PER)]
    sources = [(band * FS + my_chunk) // PER for band in range(PER)]
    barrier = pltpu.get_barrier_semaphore()

    for band in range(PER):
        for n in range(TP):
            pl.semaphore_signal(
                barrier, inc=1, device_id=(sources[band], (t + n) % TP), device_id_type=MESH
            )

    for fetch in fetches[:4]:
        fetch.wait()
    pl.semaphore_wait(barrier, PER * TP)

    def tell_targets(sem):
        for to_f in targets:
            pl.semaphore_signal(sem, inc=1, device_id=(to_f, t), device_id_type=MESH)

    tell_targets(heard_sem.at[0])

    for h in range(2):
        @pl.loop(0, PER * TP)
        def _(n):
            q = n % PER
            chunk = f * PER + q
            to_t = shifted_t(t, (n // PER) * 5 % TP)
            pltpu.make_async_remote_copy(
                src_ref=grad.at[piece(q, h, to_t)],
                dst_ref=inter[h].at[(chunk // FS) * TP + t],
                send_sem=send_sem.at[0, h],
                recv_sem=recv_sem.at[0, h],
                device_id=(swapped(chunk % FS), to_t),
                device_id_type=MESH,
            ).start()

    for fetch in fetches[4:]:
        fetch.start()

    pl.semaphore_wait(heard_sem.at[0], PER)
    tell_targets(heard_sem.at[1])

    for h in range(2):
        wait_bytes(inter[h], recv_sem.at[0, h])
        if h == 0:
            pl.semaphore_wait(heard_sem.at[1], PER)
        stage[h, me] = inter[h][owner_block[me]]
        pltpu.make_async_copy(
            stage.at[h, me], held.at[piece(my_chunk, h, t)], recv_sem.at[1, h]
        ).start()

        @pl.loop(1, OWNERS)
        def _(n):
            m = (n * 37) % OWNERS
            to_f = ((x + m // 32) % 4) * 2 + (core + m // 16) % 2
            to_t = shifted_t(t, m % TP)
            o = to_f * TP + to_t
            stage[h, o] = inter[h][owner_block[o]]
            pltpu.make_async_remote_copy(
                src_ref=stage.at[h, o],
                dst_ref=held.at[piece(my_chunk, h, t)],
                send_sem=send_sem.at[1, h],
                recv_sem=recv_sem.at[1, h],
                device_id=(to_f, to_t),
                device_id_type=MESH,
            ).start()

    fetches[4].wait()
    fetches[5].wait()

    def mix(h):
        @steps(h * HALF, (h + 1) * HALF)
        def _(cols):
            mixed[:, cols] = jnp.dot(
                left_root[...], held[:, cols], preferred_element_type=jnp.float32
            ).astype(jnp.bfloat16)

    def finish(h, cols):
        return jnp.dot(
            mixed[:, halves[h]], right_root[halves[h], cols], preferred_element_type=jnp.float32
        )

    wait_bytes(held.at[:, halves[0]], recv_sem.at[1, 0])
    mix(0)

    @steps(0, BS)
    def _(cols):
        total[:, cols] = finish(0, cols)

    wait_bytes(held.at[:, halves[1]], recv_sem.at[1, 1])
    mix(1)

    for h in range(2):
        @steps(h * HALF, (h + 1) * HALF)
        def _(cols):
            done[:, cols] = (total[:, cols] + finish(1, cols)).astype(jnp.bfloat16)

        pltpu.make_async_copy(
            done.at[piece(my_chunk, h, t)], ret[h].at[me], recv_sem.at[2, h]
        ).start()

        @pl.loop(1, OWNERS)
        def _(n):
            m = (n * 37) % OWNERS
            to_f = ((x + m // 32) % 4) * 2 + (core + m // 16) % 2
            to_t = shifted_t(t, m % TP)
            pltpu.make_async_remote_copy(
                src_ref=done.at[piece(swapped(to_f), h, to_t)],
                dst_ref=ret[h].at[me],
                send_sem=send_sem.at[2, h],
                recv_sem=recv_sem.at[2, h],
                device_id=(to_f, to_t),
                device_id_type=MESH,
            ).start()

    count = owner_count[me].astype(jnp.float32)

    def add_right():
        fetches[7].wait()

        @steps(0, BS)
        def _(rows):
            new_right[rows, :] += count * lax.dot_general(
                held[:, rows], held[...], (((0,), (0,)), ((), ())),
                preferred_element_type=jnp.float32,
            )

    def add_left():
        fetches[6].wait()

        @steps(0, BS)
        def _(rows):
            new_left[rows, :] += count * lax.dot_general(
                held[rows, :], held[...], (((1,), (1,)), ((), ())),
                preferred_element_type=jnp.float32,
            )

    for h in range(2):
        if h == 0:
            add_right()
        else:
            add_left()
        wait_bytes(ret[h], recv_sem.at[2, h])

        @pl.loop(0, NB)
        def _(n):
            band = n % PER
            to_t = shifted_t(t, (n // PER) * 5 % TP)
            b = band * TP + to_t
            chunk = band * FS + my_chunk
            back[h, b] = ret[h][block_owner[b]]
            pltpu.make_async_remote_copy(
                src_ref=back.at[h, b],
                dst_ref=update.at[piece(chunk % PER, h, t)],
                send_sem=send_sem.at[3, h],
                recv_sem=recv_sem.at[3, h],
                device_id=(chunk // PER, to_t),
                device_id_type=MESH,
            ).start()

    others = pl.ds(0, OWNERS - 1)
    for h in range(2):
        wait_bytes(inter[h], send_sem.at[0, h])
        wait_bytes(stage.at[h, others], send_sem.at[1, h])
        wait_bytes(ret[h].at[others], send_sem.at[2, h])
        wait_bytes(back.at[h], send_sem.at[3, h])
        wait_bytes(update.at[:, halves[h]], recv_sem.at[3, h])


def route(*operands):
    grad = operands[3]
    vmem = pl.BlockSpec(memory_space=pltpu.VMEM)
    stat = pltpu.VMEM((BS, BS), jnp.float32)
    square = pltpu.VMEM((BS, BS), jnp.bfloat16)
    return pl.pallas_call(
        route_kernel,
        out_shape=(stat, stat, pltpu.VMEM(grad.shape, jnp.bfloat16)),
        in_specs=[pl.BlockSpec(memory_space=pltpu.HBM)] * 8,
        out_specs=(vmem,) * 3,
        scratch_shapes=[
            pltpu.SMEM((OWNERS,), jnp.int32),
            pltpu.SMEM((NB,), jnp.int32),
            pltpu.SMEM((OWNERS,), jnp.int32),
            pltpu.VMEM(grad.shape, jnp.bfloat16),
            square,
            square,
            pltpu.VMEM((NB, RR, RC), jnp.bfloat16),
            pltpu.VMEM((NB, RR, RC), jnp.bfloat16),
            pltpu.VMEM((2, OWNERS, RR, RC), jnp.bfloat16),
            square,
            pltpu.VMEM((BS, BS), jnp.float32),
            square,
            square,
            pltpu.VMEM((OWNERS, RR, RC), jnp.bfloat16),
            pltpu.VMEM((OWNERS, RR, RC), jnp.bfloat16),
            pltpu.VMEM((2, NB, RR, RC), jnp.bfloat16),
            pltpu.SemaphoreType.DMA((8,)),
            pltpu.SemaphoreType.DMA((4, 2)),
            pltpu.SemaphoreType.DMA((4, 2)),
            pltpu.SemaphoreType.REGULAR((2,)),
        ],
        compiler_params=pltpu.CompilerParams(
            collective_id=0, has_side_effects=True, vmem_limit_bytes=40 * 1024 * 1024
        ),
        cost_estimate=pl.CostEstimate(
            flops=8 * BS**3, bytes_accessed=24 * BS * BS, transcendentals=0
        ),
        name="route",
    )(*(pltpu.with_memory_space_constraint(a, pltpu.HBM) for a in operands))


def write_kernel(left, right, update, left_out, right_out, update_out, sems):
    copies = []
    for src, dst, parts in ((left, left_out, 4), (right, right_out, 4), (update, update_out, 1)):
        rows = src.shape[0] // parts
        for i in range(parts):
            piece = pl.ds(i * rows, rows)
            copies.append(pltpu.make_async_copy(src.at[piece], dst.at[piece], sems.at[len(copies)]))
    for copy in copies:
        copy.start()
    for copy in copies:
        copy.wait()


def write(*arrays):
    return pl.pallas_call(
        write_kernel,
        out_shape=tuple(jax.ShapeDtypeStruct(a.shape, a.dtype) for a in arrays),
        in_specs=[pl.BlockSpec(memory_space=pltpu.VMEM)] * 3,
        out_specs=(pl.BlockSpec(memory_space=pltpu.HBM),) * 3,
        scratch_shapes=[pltpu.SemaphoreType.DMA((9,))],
        compiler_params=pltpu.CompilerParams(vmem_limit_bytes=1024 * 1024),
        cost_estimate=pl.CostEstimate(flops=0, bytes_accessed=18 * BS * BS, transcendentals=0),
        name="write",
    )(*(pltpu.with_memory_space_constraint(a, pltpu.VMEM) for a in arrays))


def body(grad, left_stat, right_stat, left_root, right_root, block_owner, owner_block, owner_count):
    new_left, new_right, update = write(*route(
        owner_block, block_owner, owner_count, grad,
        left_root[0], right_root[0], left_stat[0], right_stat[0],
    ))
    return new_left[None], new_right[None], update


def solution(mesh):
    whole = P(("fsdp", "tp"), None, None)
    return jax.shard_map(
        body,
        mesh=mesh,
        in_specs=(P("fsdp", "tp"), whole, whole, whole, whole, P(), P(), P()),
        out_specs=(whole, whole, P("fsdp", "tp")),
        check_vma=False,
    )
```

```python
import jax
import jax.numpy as jnp
from jax import lax
from jax.experimental import pallas as pl
from jax.experimental.pallas import tpu as pltpu
from jax.sharding import PartitionSpec as P

MESH = pl.DeviceIdType.MESH
BS = 1024
HALF = BS // 2
FS = 8
TP = 16
NB = 48
OWNERS = FS * TP
CHUNK = BS // FS
RR, RC = 16, 256
PER = 3
STEP = 256


def piece(chunk, half, t):
    return (
        pl.ds(pl.multiple_of(chunk * CHUNK + (t // 2) * RR, RR), RR),
        pl.ds(pl.multiple_of(half * HALF + (t % 2) * RC, RC), RC),
    )


def swapped(k):
    return (k // 4) * 4 + 3 - k % 4


def shifted_t(t, n):
    return ((t // 4 + n // 4) % 4) * 4 + (t % 4 + n % 4) % 4


def wait_bytes(ref, sem):
    pltpu.make_async_copy(ref, ref, sem).wait()


def steps(first, last):
    def over(fn):
        @pl.loop(first // STEP, last // STEP)
        def _(c):
            fn(pl.ds(pl.multiple_of(c * STEP, STEP), STEP))

    return over


def route_kernel(
    owner_block_any, block_owner_any, owner_count_any, grad_any,
    left_root_any, right_root_any, left_stat_any, right_stat_any,
    new_left, new_right, update,
    owner_block, block_owner, owner_count, grad, left_root, right_root,
    inter_0, inter_1, stage, held, total, mixed, done, ret_0, ret_1, back,
    local_sem, send_sem, recv_sem, heard_sem,
):
    f = lax.axis_index("fsdp")
    t = lax.axis_index("tp")
    me = f * TP + t
    x, core = f // 2, f % 2
    my_chunk = swapped(f)
    inter, ret = (inter_0, inter_1), (ret_0, ret_1)
    halves = [pl.ds(h * HALF, HALF) for h in range(2)]

    fetches = [
        pltpu.make_async_copy(src, dst, local_sem.at[i])
        for i, (src, dst) in enumerate((
            (owner_block_any, owner_block),
            (block_owner_any, block_owner),
            (owner_count_any, owner_count),
            (grad_any, grad),
            (left_root_any, left_root),
            (right_root_any, right_root),
            (left_stat_any, new_left),
            (right_stat_any, new_right),
        ))
    ]
    for fetch in fetches[:4]:
        fetch.start()

    targets = [swapped((f * PER + q) % FS) for q in range(PER)]
    sources = [(band * FS + my_chunk) // PER for band in range(PER)]
    barrier = pltpu.get_barrier_semaphore()

    for band in range(PER):
        for n in range(TP):
            pl.semaphore_signal(
                barrier, inc=1, device_id=(sources[band], (t + n) % TP), device_id_type=MESH
            )

    for fetch in fetches[:4]:
        fetch.wait()
    pl.semaphore_wait(barrier, PER * TP)

    def tell_targets(sem):
        for to_f in targets:
            pl.semaphore_signal(sem, inc=1, device_id=(to_f, t), device_id_type=MESH)

    tell_targets(heard_sem.at[0])

    for h in range(2):
        @pl.loop(0, PER * TP)
        def _(n):
            q = n % PER
            chunk = f * PER + q
            to_t = shifted_t(t, (n // PER) * 5 % TP)
            pltpu.make_async_remote_copy(
                src_ref=grad.at[piece(q, h, to_t)],
                dst_ref=inter[h].at[(chunk // FS) * TP + t],
                send_sem=send_sem.at[0, h],
                recv_sem=recv_sem.at[0, h],
                device_id=(swapped(chunk % FS), to_t),
                device_id_type=MESH,
            ).start()

    for fetch in fetches[4:]:
        fetch.start()

    pl.semaphore_wait(heard_sem.at[0], PER)
    tell_targets(heard_sem.at[1])

    for to_core in range(2):
        for h in range(2):
            if to_core == 0:
                wait_bytes(inter[h], recv_sem.at[0, h])
                if h == 0:
                    pl.semaphore_wait(heard_sem.at[1], PER)

            def serve(n):
                to_f = ((x + n // TP) % 4) * 2 + to_core
                to_t = shifted_t(t, n % TP)
                o = to_f * TP + to_t
                stage[h, o] = inter[h][owner_block[o]]
                pltpu.make_async_remote_copy(
                    src_ref=stage.at[h, o],
                    dst_ref=held.at[piece(my_chunk, h, t)],
                    send_sem=send_sem.at[1, h],
                    recv_sem=recv_sem.at[1, h],
                    device_id=(to_f, to_t),
                    device_id_type=MESH,
                ).start()

            @pl.when(core == to_core)
            def _():
                stage[h, me] = inter[h][owner_block[me]]
                pltpu.make_async_copy(
                    stage.at[h, me], held.at[piece(my_chunk, h, t)], recv_sem.at[1, h]
                ).start()

            @pl.when(core != to_core)
            def _():
                serve(0)

            @pl.loop(1, OWNERS // 2)
            def _(n):
                serve((n * 37) % (OWNERS // 2))

    fetches[4].wait()
    fetches[5].wait()

    def mix(h):
        @steps(h * HALF, (h + 1) * HALF)
        def _(cols):
            mixed[:, cols] = jnp.dot(
                left_root[...], held[:, cols], preferred_element_type=jnp.float32
            ).astype(jnp.bfloat16)

    def finish(h, cols):
        return jnp.dot(
            mixed[:, halves[h]], right_root[halves[h], cols], preferred_element_type=jnp.float32
        )

    wait_bytes(held.at[:, halves[0]], recv_sem.at[1, 0])
    mix(0)

    @steps(0, BS)
    def _(cols):
        total[:, cols] = finish(0, cols)

    wait_bytes(held.at[:, halves[1]], recv_sem.at[1, 1])
    mix(1)

    for h in range(2):
        @steps(h * HALF, (h + 1) * HALF)
        def _(cols):
            done[:, cols] = (total[:, cols] + finish(1, cols)).astype(jnp.bfloat16)

        pltpu.make_async_copy(
            done.at[piece(my_chunk, h, t)], ret[h].at[me], recv_sem.at[2, h]
        ).start()

        @pl.loop(1, OWNERS)
        def _(n):
            m = (n * 37) % OWNERS
            to_f = ((x + m // 32) % 4) * 2 + (core + m // 16) % 2
            to_t = shifted_t(t, m % TP)
            pltpu.make_async_remote_copy(
                src_ref=done.at[piece(swapped(to_f), h, to_t)],
                dst_ref=ret[h].at[me],
                send_sem=send_sem.at[2, h],
                recv_sem=recv_sem.at[2, h],
                device_id=(to_f, to_t),
                device_id_type=MESH,
            ).start()

    count = owner_count[me].astype(jnp.float32)

    def add_right():
        fetches[7].wait()

        @steps(0, BS)
        def _(rows):
            new_right[rows, :] += count * lax.dot_general(
                held[:, rows], held[...], (((0,), (0,)), ((), ())),
                preferred_element_type=jnp.float32,
            )

    def add_left():
        fetches[6].wait()

        @steps(0, BS)
        def _(rows):
            new_left[rows, :] += count * lax.dot_general(
                held[rows, :], held[...], (((1,), (1,)), ((), ())),
                preferred_element_type=jnp.float32,
            )

    for h in range(2):
        if h == 0:
            add_right()
        else:
            add_left()
        wait_bytes(ret[h], recv_sem.at[2, h])

        @pl.loop(0, NB)
        def _(n):
            band = n % PER
            to_t = shifted_t(t, (n // PER) * 5 % TP)
            b = band * TP + to_t
            chunk = band * FS + my_chunk
            back[h, b] = ret[h][block_owner[b]]
            pltpu.make_async_remote_copy(
                src_ref=back.at[h, b],
                dst_ref=update.at[piece(chunk % PER, h, t)],
                send_sem=send_sem.at[3, h],
                recv_sem=recv_sem.at[3, h],
                device_id=(chunk // PER, to_t),
                device_id_type=MESH,
            ).start()

    others = pl.ds(0, OWNERS - 1)
    for h in range(2):
        wait_bytes(inter[h], send_sem.at[0, h])
        wait_bytes(stage.at[h, others], send_sem.at[1, h])
        wait_bytes(ret[h].at[others], send_sem.at[2, h])
        wait_bytes(back.at[h], send_sem.at[3, h])
        wait_bytes(update.at[:, halves[h]], recv_sem.at[3, h])


def route(*operands):
    grad = operands[3]
    vmem = pl.BlockSpec(memory_space=pltpu.VMEM)
    stat = pltpu.VMEM((BS, BS), jnp.float32)
    square = pltpu.VMEM((BS, BS), jnp.bfloat16)
    return pl.pallas_call(
        route_kernel,
        out_shape=(stat, stat, pltpu.VMEM(grad.shape, jnp.bfloat16)),
        in_specs=[pl.BlockSpec(memory_space=pltpu.HBM)] * 8,
        out_specs=(vmem,) * 3,
        scratch_shapes=[
            pltpu.SMEM((OWNERS,), jnp.int32),
            pltpu.SMEM((NB,), jnp.int32),
            pltpu.SMEM((OWNERS,), jnp.int32),
            pltpu.VMEM(grad.shape, jnp.bfloat16),
            square,
            square,
            pltpu.VMEM((NB, RR, RC), jnp.bfloat16),
            pltpu.VMEM((NB, RR, RC), jnp.bfloat16),
            pltpu.VMEM((2, OWNERS, RR, RC), jnp.bfloat16),
            square,
            pltpu.VMEM((BS, BS), jnp.float32),
            square,
            square,
            pltpu.VMEM((OWNERS, RR, RC), jnp.bfloat16),
            pltpu.VMEM((OWNERS, RR, RC), jnp.bfloat16),
            pltpu.VMEM((2, NB, RR, RC), jnp.bfloat16),
            pltpu.SemaphoreType.DMA((8,)),
            pltpu.SemaphoreType.DMA((4, 2)),
            pltpu.SemaphoreType.DMA((4, 2)),
            pltpu.SemaphoreType.REGULAR((2,)),
        ],
        compiler_params=pltpu.CompilerParams(
            collective_id=0, has_side_effects=True, vmem_limit_bytes=40 * 1024 * 1024
        ),
        cost_estimate=pl.CostEstimate(
            flops=8 * BS**3, bytes_accessed=24 * BS * BS, transcendentals=0
        ),
        name="route",
    )(*(pltpu.with_memory_space_constraint(a, pltpu.HBM) for a in operands))


def write_kernel(left, right, update, left_out, right_out, update_out, sems):
    copies = []
    for src, dst, parts in ((left, left_out, 4), (right, right_out, 4), (update, update_out, 1)):
        rows = src.shape[0] // parts
        for i in range(parts):
            piece = pl.ds(i * rows, rows)
            copies.append(pltpu.make_async_copy(src.at[piece], dst.at[piece], sems.at[len(copies)]))
    for copy in copies:
        copy.start()
    for copy in copies:
        copy.wait()


def write(*arrays):
    return pl.pallas_call(
        write_kernel,
        out_shape=tuple(jax.ShapeDtypeStruct(a.shape, a.dtype) for a in arrays),
        in_specs=[pl.BlockSpec(memory_space=pltpu.VMEM)] * 3,
        out_specs=(pl.BlockSpec(memory_space=pltpu.HBM),) * 3,
        scratch_shapes=[pltpu.SemaphoreType.DMA((9,))],
        compiler_params=pltpu.CompilerParams(vmem_limit_bytes=1024 * 1024),
        cost_estimate=pl.CostEstimate(flops=0, bytes_accessed=18 * BS * BS, transcendentals=0),
        name="write",
    )(*(pltpu.with_memory_space_constraint(a, pltpu.VMEM) for a in arrays))


def body(grad, left_stat, right_stat, left_root, right_root, block_owner, owner_block, owner_count):
    new_left, new_right, update = write(*route(
        owner_block, block_owner, owner_count, grad,
        left_root[0], right_root[0], left_stat[0], right_stat[0],
    ))
    return new_left[None], new_right[None], update


def solution(mesh):
    whole = P(("fsdp", "tp"), None, None)
    return jax.shard_map(
        body,
        mesh=mesh,
        in_specs=(P("fsdp", "tp"), whole, whole, whole, whole, P(), P(), P()),
        out_specs=(whole, whole, P("fsdp", "tp")),
        check_vma=False,
    )
```

```python
import jax
import jax.numpy as jnp
from jax import lax
from jax.experimental import pallas as pl
from jax.experimental.pallas import tpu as pltpu
from jax.sharding import PartitionSpec as P

MESH = pl.DeviceIdType.MESH
BS = 1024
FS = 8
TP = 16
NB = 48
OWNERS = FS * TP
CHUNK = BS // FS
PER = 3
STEP = 256
RR = 16
IN = (512, 512)
OUT = (768, 256)


def part_cols(parts, h):
    return pl.ds(sum(parts[:h]), parts[h])


def piece(chunk, parts, h, t):
    width = parts[h] // 2
    return (
        pl.ds(pl.multiple_of(chunk * CHUNK + lax.div(t, 2) * RR, RR), RR),
        pl.ds(pl.multiple_of(sum(parts[:h]) + lax.rem(t, 2) * width, 128), width),
    )


def swapped(k):
    return lax.div(k, 4) * 4 + 3 - lax.rem(k, 4)


def shifted_t(t, n):
    y = lax.rem(lax.div(t, 4) + lax.div(n, 4), 4)
    return y * 4 + lax.rem(t + n, 4)


def wait_bytes(ref, sem):
    pltpu.make_async_copy(ref, ref, sem).wait()


def steps(parts, h):
    def over(fn):
        first = sum(parts[:h]) // STEP

        @pl.loop(first, first + parts[h] // STEP)
        def _(c):
            fn(pl.ds(pl.multiple_of(c * STEP, STEP), STEP))

    return over


def route_kernel(
    owner_block_any, block_owner_any, owner_count_any, grad_any,
    left_root_any, right_root_any, left_stat_any, right_stat_any,
    new_left, new_right, update,
    owner_block, block_owner, owner_count, grad, left_root, right_root,
    inter_0, inter_1, stage_0, stage_1, held, total, mixed, done, ret_0, ret_1, back_0, back_1,
    local_sem, send_sem, recv_sem, heard_sem,
):
    f = lax.axis_index("fsdp")
    t = lax.axis_index("tp")
    me = f * TP + t
    x, core = f // 2, f % 2
    my_chunk = swapped(f)
    inter, stage = (inter_0, inter_1), (stage_0, stage_1)
    ret, back = (ret_0, ret_1), (back_0, back_1)

    fetches = [
        pltpu.make_async_copy(src, dst, local_sem.at[i])
        for i, (src, dst) in enumerate((
            (owner_block_any, owner_block),
            (block_owner_any, block_owner),
            (owner_count_any, owner_count),
            (grad_any, grad),
            (left_root_any, left_root),
            (right_root_any, right_root),
            (left_stat_any, new_left),
            (right_stat_any, new_right),
        ))
    ]
    fetches[3].start()

    targets = [swapped((f * PER + q) % FS) for q in range(PER)]
    sources = [(band * FS + my_chunk) // PER for band in range(PER)]
    spread_to = [(f * PER + q) // FS * TP + t for q in range(PER)]
    barrier = pltpu.get_barrier_semaphore()

    for band in range(PER):
        for n in range(TP):
            pl.semaphore_signal(
                barrier, inc=1, device_id=(sources[band], (t + n) % TP), device_id_type=MESH
            )

    fetches[3].wait()
    pl.semaphore_wait(barrier, PER * TP)

    def tell_targets(sem):
        for to_f in targets:
            pl.semaphore_signal(sem, inc=1, device_id=(to_f, t), device_id_type=MESH)

    tell_targets(heard_sem.at[0])

    for h in range(2):
        @pl.loop(0, TP)
        def _(n):
            to_t = shifted_t(t, lax.rem(n * 5, TP))
            for q in range(PER):
                pltpu.make_async_remote_copy(
                    src_ref=grad.at[piece(q, IN, h, to_t)],
                    dst_ref=inter[h].at[spread_to[q]],
                    send_sem=send_sem.at[0, h],
                    recv_sem=recv_sem.at[0, h],
                    device_id=(targets[q], to_t),
                    device_id_type=MESH,
                ).start()

    for i in (0, 1, 2, 4, 5, 6, 7):
        fetches[i].start()

    pl.semaphore_wait(heard_sem.at[0], PER)
    tell_targets(heard_sem.at[1])
    for fetch in fetches[:3]:
        fetch.wait()

    for to_core in range(2):
        for h in range(2):
            if to_core == 0:
                wait_bytes(inter[h], recv_sem.at[0, h])
                if h == 0:
                    pl.semaphore_wait(heard_sem.at[1], PER)

            def serve(n):
                to_f = lax.rem(x + lax.div(n, TP), 4) * 2 + to_core
                to_t = shifted_t(t, lax.rem(n, TP))
                o = to_f * TP + to_t
                stage[h][o] = inter[h][owner_block[o]]
                pltpu.make_async_remote_copy(
                    src_ref=stage[h].at[o],
                    dst_ref=held.at[piece(my_chunk, IN, h, t)],
                    send_sem=send_sem.at[1, h],
                    recv_sem=recv_sem.at[1, h],
                    device_id=(to_f, to_t),
                    device_id_type=MESH,
                ).start()

            @pl.when(core == to_core)
            def _():
                stage[h][me] = inter[h][owner_block[me]]
                pltpu.make_async_copy(
                    stage[h].at[me], held.at[piece(my_chunk, IN, h, t)], recv_sem.at[1, h]
                ).start()

            @pl.when(core != to_core)
            def _():
                serve(jnp.int32(0))

            @pl.loop(1, OWNERS // 2)
            def _(n):
                serve(lax.rem(n * 37, OWNERS // 2))

    fetches[4].wait()
    fetches[5].wait()

    def mix(h):
        @steps(IN, h)
        def _(cols):
            mixed[:, cols] = jnp.dot(
                left_root[...], held[:, cols], preferred_element_type=jnp.float32
            ).astype(jnp.bfloat16)

    def finish(h, cols):
        rows = part_cols(IN, h)
        return jnp.dot(
            mixed[:, rows], right_root[rows, cols], preferred_element_type=jnp.float32
        )

    wait_bytes(held.at[:, part_cols(IN, 0)], recv_sem.at[1, 0])
    mix(0)

    @steps((BS,), 0)
    def _(cols):
        total[:, cols] = finish(0, cols)

    wait_bytes(held.at[:, part_cols(IN, 1)], recv_sem.at[1, 1])
    mix(1)

    for h in range(2):
        @steps(OUT, h)
        def _(cols):
            done[:, cols] = (total[:, cols] + finish(1, cols)).astype(jnp.bfloat16)

        pltpu.make_async_copy(
            done.at[piece(my_chunk, OUT, h, t)], ret[h].at[me], recv_sem.at[2, h]
        ).start()

        @pl.loop(1, OWNERS)
        def _(n):
            m = lax.rem(n * 37, OWNERS)
            to_f = lax.rem(x + lax.div(m, 32), 4) * 2 + lax.rem(core + lax.div(m, TP), 2)
            to_t = shifted_t(t, lax.rem(m, TP))
            pltpu.make_async_remote_copy(
                src_ref=done.at[piece(swapped(to_f), OUT, h, to_t)],
                dst_ref=ret[h].at[me],
                send_sem=send_sem.at[2, h],
                recv_sem=recv_sem.at[2, h],
                device_id=(to_f, to_t),
                device_id_type=MESH,
            ).start()

    count = owner_count[me].astype(jnp.float32)

    def add_statistics():
        for sem, stat, axis in ((7, new_right, 0), (6, new_left, 1)):
            fetches[sem].wait()

            @steps((BS,), 0)
            def _(some):
                lhs = held[:, some] if axis == 0 else held[some, :]
                stat[some, :] += count * lax.dot_general(
                    lhs, held[...], (((axis,), (axis,)), ((), ())),
                    preferred_element_type=jnp.float32,
                )

    pl.when(core == 0)(add_statistics)

    for h in range(2):
        wait_bytes(ret[h], recv_sem.at[2, h])

        @pl.loop(0, TP)
        def _(n):
            to_t = shifted_t(t, lax.rem(n * 5, TP))
            for band in range(PER):
                b = band * TP + to_t
                back[h][b] = ret[h][block_owner[b]]
                pltpu.make_async_remote_copy(
                    src_ref=back[h].at[b],
                    dst_ref=update.at[piece((band * FS + my_chunk) % PER, OUT, h, t)],
                    send_sem=send_sem.at[3, h],
                    recv_sem=recv_sem.at[3, h],
                    device_id=(sources[band], to_t),
                    device_id_type=MESH,
                ).start()

    pl.when(core == 1)(add_statistics)

    others = pl.ds(0, OWNERS - 1)
    for h in range(2):
        wait_bytes(inter[h], send_sem.at[0, h])
        wait_bytes(stage[h].at[others], send_sem.at[1, h])
        wait_bytes(ret[h].at[others], send_sem.at[2, h])
        wait_bytes(back[h], send_sem.at[3, h])
        wait_bytes(update.at[:, part_cols(OUT, h)], recv_sem.at[3, h])


def route(*operands):
    grad = operands[3]
    vmem = pl.BlockSpec(memory_space=pltpu.VMEM)
    stat = pltpu.VMEM((BS, BS), jnp.float32)
    square = pltpu.VMEM((BS, BS), jnp.bfloat16)
    return pl.pallas_call(
        route_kernel,
        out_shape=(stat, stat, pltpu.VMEM(grad.shape, jnp.bfloat16)),
        in_specs=[pl.BlockSpec(memory_space=pltpu.HBM)] * 8,
        out_specs=(vmem,) * 3,
        scratch_shapes=[
            pltpu.SMEM((OWNERS,), jnp.int32),
            pltpu.SMEM((NB,), jnp.int32),
            pltpu.SMEM((OWNERS,), jnp.int32),
            pltpu.VMEM(grad.shape, jnp.bfloat16),
            square,
            square,
            *[pltpu.VMEM((NB, RR, w // 2), jnp.bfloat16) for w in IN],
            *[pltpu.VMEM((OWNERS, RR, w // 2), jnp.bfloat16) for w in IN],
            square,
            pltpu.VMEM((BS, BS), jnp.float32),
            square,
            square,
            *[pltpu.VMEM((OWNERS, RR, w // 2), jnp.bfloat16) for w in OUT],
            *[pltpu.VMEM((NB, RR, w // 2), jnp.bfloat16) for w in OUT],
            pltpu.SemaphoreType.DMA((8,)),
            pltpu.SemaphoreType.DMA((4, 2)),
            pltpu.SemaphoreType.DMA((4, 2)),
            pltpu.SemaphoreType.REGULAR((2,)),
        ],
        compiler_params=pltpu.CompilerParams(
            collective_id=0, has_side_effects=True, vmem_limit_bytes=40 * 1024 * 1024
        ),
        cost_estimate=pl.CostEstimate(
            flops=8 * BS**3, bytes_accessed=24 * BS * BS, transcendentals=0
        ),
        name="route",
    )(*(pltpu.with_memory_space_constraint(a, pltpu.HBM) for a in operands))


def write_kernel(left, right, update, left_out, right_out, update_out, sems):
    copies = []
    for src, dst, parts in ((left, left_out, 4), (right, right_out, 4), (update, update_out, 1)):
        rows = src.shape[0] // parts
        for i in range(parts):
            piece = pl.ds(i * rows, rows)
            copies.append(pltpu.make_async_copy(src.at[piece], dst.at[piece], sems.at[len(copies)]))
    for copy in copies:
        copy.start()
    for copy in copies:
        copy.wait()


def write(*arrays):
    return pl.pallas_call(
        write_kernel,
        out_shape=tuple(jax.ShapeDtypeStruct(a.shape, a.dtype) for a in arrays),
        in_specs=[pl.BlockSpec(memory_space=pltpu.VMEM)] * 3,
        out_specs=(pl.BlockSpec(memory_space=pltpu.HBM),) * 3,
        scratch_shapes=[pltpu.SemaphoreType.DMA((9,))],
        compiler_params=pltpu.CompilerParams(vmem_limit_bytes=1024 * 1024),
        cost_estimate=pl.CostEstimate(flops=0, bytes_accessed=18 * BS * BS, transcendentals=0),
        name="write",
    )(*(pltpu.with_memory_space_constraint(a, pltpu.VMEM) for a in arrays))


def body(grad, left_stat, right_stat, left_root, right_root, block_owner, owner_block, owner_count):
    new_left, new_right, update = write(*route(
        owner_block, block_owner, owner_count, grad,
        left_root[0], right_root[0], left_stat[0], right_stat[0],
    ))
    return new_left[None], new_right[None], update


def solution(mesh):
    whole = P(("fsdp", "tp"), None, None)
    return jax.shard_map(
        body,
        mesh=mesh,
        in_specs=(P("fsdp", "tp"), whole, whole, whole, whole, P(), P(), P()),
        out_specs=(whole, whole, P("fsdp", "tp")),
        check_vma=False,
    )
```

```python
import jax
import jax.numpy as jnp
from jax import lax
from jax.experimental import pallas as pl
from jax.experimental.pallas import tpu as pltpu
from jax.sharding import PartitionSpec as P

MESH = pl.DeviceIdType.MESH
BS = 1024
FS = 8
TP = 16
NB = 48
OWNERS = FS * TP
CHUNK = BS // FS
PER = 3
STEP = 256
RR = 16
IN = (512, 512)
OUT = (768, 256)


def part_cols(parts, h):
    return pl.ds(sum(parts[:h]), parts[h])


def piece(chunk, parts, h, t):
    width = parts[h] // 2
    return (
        pl.ds(pl.multiple_of(chunk * CHUNK + lax.div(t, 2) * RR, RR), RR),
        pl.ds(pl.multiple_of(sum(parts[:h]) + lax.rem(t, 2) * width, 128), width),
    )


def swapped(k):
    return lax.div(k, 4) * 4 + 3 - lax.rem(k, 4)


def shifted_t(t, n):
    y = lax.rem(lax.div(t, 4) + lax.div(n, 4), 4)
    return y * 4 + lax.rem(t + n, 4)


def wait_bytes(ref, sem):
    pltpu.make_async_copy(ref, ref, sem).wait()


def steps(parts, h):
    def over(fn):
        first = sum(parts[:h]) // STEP

        @pl.loop(first, first + parts[h] // STEP)
        def _(c):
            fn(pl.ds(pl.multiple_of(c * STEP, STEP), STEP))

    return over


def route_kernel(
    owner_block_any, block_owner_any, owner_count_any, grad_any,
    left_root_any, right_root_any, left_stat_any, right_stat_any,
    new_left, new_right, update,
    owner_block, block_owner, owner_count, grad, left_root, right_root,
    inter_0, inter_1, stage_0, stage_1, held, total, mixed, done, ret_0, ret_1, back_0, back_1,
    local_sem, send_sem, recv_sem, heard_sem,
):
    f = lax.axis_index("fsdp")
    t = lax.axis_index("tp")
    me = f * TP + t
    x, core = f // 2, f % 2
    my_chunk = swapped(f)
    inter, stage = (inter_0, inter_1), (stage_0, stage_1)
    ret, back = (ret_0, ret_1), (back_0, back_1)

    fetches = [
        pltpu.make_async_copy(src, dst, local_sem.at[i])
        for i, (src, dst) in enumerate((
            (owner_block_any, owner_block),
            (block_owner_any, block_owner),
            (owner_count_any, owner_count),
            (grad_any, grad),
            (left_root_any, left_root),
            (right_root_any, right_root),
            (left_stat_any, new_left),
            (right_stat_any, new_right),
        ))
    ]
    fetches[3].start()

    targets = [swapped((f * PER + q) % FS) for q in range(PER)]
    sources = [(band * FS + my_chunk) // PER for band in range(PER)]
    spread_to = [(f * PER + q) // FS * TP + t for q in range(PER)]
    barrier = pltpu.get_barrier_semaphore()

    for band in range(PER):
        for n in range(TP):
            pl.semaphore_signal(
                barrier, inc=1, device_id=(sources[band], (t + n) % TP), device_id_type=MESH
            )

    fetches[3].wait()
    pl.semaphore_wait(barrier, PER * TP)

    def tell_targets(sem):
        for to_f in targets:
            pl.semaphore_signal(sem, inc=1, device_id=(to_f, t), device_id_type=MESH)

    tell_targets(heard_sem.at[0])

    for h in range(2):
        @pl.loop(0, TP)
        def _(n):
            to_t = shifted_t(t, lax.rem(n * 5, TP))
            for q in range(PER):
                pltpu.make_async_remote_copy(
                    src_ref=grad.at[piece(q, IN, h, to_t)],
                    dst_ref=inter[h].at[spread_to[q]],
                    send_sem=send_sem.at[0, h],
                    recv_sem=recv_sem.at[0, h],
                    device_id=(targets[q], to_t),
                    device_id_type=MESH,
                ).start()

    for i in (0, 1, 2, 4, 5, 6, 7):
        fetches[i].start()

    pl.semaphore_wait(heard_sem.at[0], PER)
    tell_targets(heard_sem.at[1])
    for fetch in fetches[:3]:
        fetch.wait()

    for to_core in range(2):
        for h in range(2):
            if to_core == 0:
                wait_bytes(inter[h], recv_sem.at[0, h])
                if h == 0:
                    pl.semaphore_wait(heard_sem.at[1], PER)

            def serve(n):
                to_f = lax.rem(x + lax.div(n, TP), 4) * 2 + to_core
                to_t = shifted_t(t, lax.rem(n, TP))
                o = to_f * TP + to_t
                stage[h][o] = inter[h][owner_block[o]]
                pltpu.make_async_remote_copy(
                    src_ref=stage[h].at[o],
                    dst_ref=held.at[piece(my_chunk, IN, h, t)],
                    send_sem=send_sem.at[1, h],
                    recv_sem=recv_sem.at[1, h],
                    device_id=(to_f, to_t),
                    device_id_type=MESH,
                ).start()

            @pl.when(core == to_core)
            def _():
                stage[h][me] = inter[h][owner_block[me]]
                pltpu.make_async_copy(
                    stage[h].at[me], held.at[piece(my_chunk, IN, h, t)], recv_sem.at[1, h]
                ).start()

            @pl.when(core != to_core)
            def _():
                serve(jnp.int32(0))

            @pl.loop(1, OWNERS // 2)
            def _(n):
                serve(lax.rem(n * 53, OWNERS // 2))

    fetches[4].wait()
    fetches[5].wait()

    def mix(h):
        @steps(IN, h)
        def _(cols):
            mixed[:, cols] = jnp.dot(
                left_root[...], held[:, cols], preferred_element_type=jnp.float32
            ).astype(jnp.bfloat16)

    def finish(h, cols):
        rows = part_cols(IN, h)
        return jnp.dot(
            mixed[:, rows], right_root[rows, cols], preferred_element_type=jnp.float32
        )

    wait_bytes(held.at[:, part_cols(IN, 0)], recv_sem.at[1, 0])
    mix(0)

    @steps((BS,), 0)
    def _(cols):
        total[:, cols] = finish(0, cols)

    wait_bytes(held.at[:, part_cols(IN, 1)], recv_sem.at[1, 1])
    mix(1)

    for h in range(2):
        @steps(OUT, h)
        def _(cols):
            done[:, cols] = (total[:, cols] + finish(1, cols)).astype(jnp.bfloat16)

        pltpu.make_async_copy(
            done.at[piece(my_chunk, OUT, h, t)], ret[h].at[me], recv_sem.at[2, h]
        ).start()

        @pl.loop(1, OWNERS)
        def _(n):
            m = lax.rem(n * 69, OWNERS)
            to_f = lax.rem(x + lax.div(m, 32), 4) * 2 + lax.rem(core + lax.div(m, TP), 2)
            to_t = shifted_t(t, lax.rem(m, TP))
            pltpu.make_async_remote_copy(
                src_ref=done.at[piece(swapped(to_f), OUT, h, to_t)],
                dst_ref=ret[h].at[me],
                send_sem=send_sem.at[2, h],
                recv_sem=recv_sem.at[2, h],
                device_id=(to_f, to_t),
                device_id_type=MESH,
            ).start()

    count = owner_count[me].astype(jnp.float32)

    def add_statistics():
        for sem, stat, axis in ((7, new_right, 0), (6, new_left, 1)):
            fetches[sem].wait()

            @steps((BS,), 0)
            def _(some):
                lhs = held[:, some] if axis == 0 else held[some, :]
                stat[some, :] += count * lax.dot_general(
                    lhs, held[...], (((axis,), (axis,)), ((), ())),
                    preferred_element_type=jnp.float32,
                )

    pl.when(core == 0)(add_statistics)

    for h in range(2):
        wait_bytes(ret[h], recv_sem.at[2, h])

        @pl.loop(0, TP)
        def _(n):
            to_t = shifted_t(t, lax.rem(n * 5, TP))
            for band in range(PER):
                b = band * TP + to_t
                back[h][b] = ret[h][block_owner[b]]
                pltpu.make_async_remote_copy(
                    src_ref=back[h].at[b],
                    dst_ref=update.at[piece((band * FS + my_chunk) % PER, OUT, h, t)],
                    send_sem=send_sem.at[3, h],
                    recv_sem=recv_sem.at[3, h],
                    device_id=(sources[band], to_t),
                    device_id_type=MESH,
                ).start()

    pl.when(core == 1)(add_statistics)

    others = pl.ds(0, OWNERS - 1)
    for h in range(2):
        wait_bytes(inter[h], send_sem.at[0, h])
        wait_bytes(stage[h].at[others], send_sem.at[1, h])
        wait_bytes(ret[h].at[others], send_sem.at[2, h])
        wait_bytes(back[h], send_sem.at[3, h])
        wait_bytes(update.at[:, part_cols(OUT, h)], recv_sem.at[3, h])


def route(*operands):
    grad = operands[3]
    vmem = pl.BlockSpec(memory_space=pltpu.VMEM)
    stat = pltpu.VMEM((BS, BS), jnp.float32)
    square = pltpu.VMEM((BS, BS), jnp.bfloat16)
    return pl.pallas_call(
        route_kernel,
        out_shape=(stat, stat, pltpu.VMEM(grad.shape, jnp.bfloat16)),
        in_specs=[pl.BlockSpec(memory_space=pltpu.HBM)] * 8,
        out_specs=(vmem,) * 3,
        scratch_shapes=[
            pltpu.SMEM((OWNERS,), jnp.int32),
            pltpu.SMEM((NB,), jnp.int32),
            pltpu.SMEM((OWNERS,), jnp.int32),
            pltpu.VMEM(grad.shape, jnp.bfloat16),
            square,
            square,
            *[pltpu.VMEM((NB, RR, w // 2), jnp.bfloat16) for w in IN],
            *[pltpu.VMEM((OWNERS, RR, w // 2), jnp.bfloat16) for w in IN],
            square,
            pltpu.VMEM((BS, BS), jnp.float32),
            square,
            square,
            *[pltpu.VMEM((OWNERS, RR, w // 2), jnp.bfloat16) for w in OUT],
            *[pltpu.VMEM((NB, RR, w // 2), jnp.bfloat16) for w in OUT],
            pltpu.SemaphoreType.DMA((8,)),
            pltpu.SemaphoreType.DMA((4, 2)),
            pltpu.SemaphoreType.DMA((4, 2)),
            pltpu.SemaphoreType.REGULAR((2,)),
        ],
        compiler_params=pltpu.CompilerParams(
            collective_id=0, has_side_effects=True, vmem_limit_bytes=40 * 1024 * 1024
        ),
        cost_estimate=pl.CostEstimate(
            flops=8 * BS**3, bytes_accessed=24 * BS * BS, transcendentals=0
        ),
        name="route",
    )(*(pltpu.with_memory_space_constraint(a, pltpu.HBM) for a in operands))


def write_kernel(left, right, update, left_out, right_out, update_out, sems):
    copies = []
    for src, dst, parts in ((left, left_out, 4), (right, right_out, 4), (update, update_out, 1)):
        rows = src.shape[0] // parts
        for i in range(parts):
            piece = pl.ds(i * rows, rows)
            copies.append(pltpu.make_async_copy(src.at[piece], dst.at[piece], sems.at[len(copies)]))
    for copy in copies:
        copy.start()
    for copy in copies:
        copy.wait()


def write(*arrays):
    return pl.pallas_call(
        write_kernel,
        out_shape=tuple(jax.ShapeDtypeStruct(a.shape, a.dtype) for a in arrays),
        in_specs=[pl.BlockSpec(memory_space=pltpu.VMEM)] * 3,
        out_specs=(pl.BlockSpec(memory_space=pltpu.HBM),) * 3,
        scratch_shapes=[pltpu.SemaphoreType.DMA((9,))],
        compiler_params=pltpu.CompilerParams(vmem_limit_bytes=1024 * 1024),
        cost_estimate=pl.CostEstimate(flops=0, bytes_accessed=18 * BS * BS, transcendentals=0),
        name="write",
    )(*(pltpu.with_memory_space_constraint(a, pltpu.VMEM) for a in arrays))


def body(grad, left_stat, right_stat, left_root, right_root, block_owner, owner_block, owner_count):
    new_left, new_right, update = write(*route(
        owner_block, block_owner, owner_count, grad,
        left_root[0], right_root[0], left_stat[0], right_stat[0],
    ))
    return new_left[None], new_right[None], update


def solution(mesh):
    whole = P(("fsdp", "tp"), None, None)
    return jax.shard_map(
        body,
        mesh=mesh,
        in_specs=(P("fsdp", "tp"), whole, whole, whole, whole, P(), P(), P()),
        out_specs=(whole, whole, P("fsdp", "tp")),
        check_vma=False,
    )
```

```python
import jax
import jax.numpy as jnp
from jax import lax
from jax.experimental import pallas as pl
from jax.experimental.pallas import tpu as pltpu
from jax.sharding import PartitionSpec as P

MESH = pl.DeviceIdType.MESH
BS = 1024
FS = 8
TP = 16
NB = 48
OWNERS = FS * TP
CHUNK = BS // FS
PER = 3
STEP = 256
RR = 16
IN = (512, 512)
OUT = (768, 256)


def part_cols(parts, h):
    return pl.ds(sum(parts[:h]), parts[h])


def piece(chunk, parts, h, t):
    width = parts[h] // 2
    return (
        pl.ds(pl.multiple_of(chunk * CHUNK + lax.div(t, 2) * RR, RR), RR),
        pl.ds(pl.multiple_of(sum(parts[:h]) + lax.rem(t, 2) * width, 128), width),
    )


def swapped(k):
    return lax.div(k, 4) * 4 + 3 - lax.rem(k, 4)


def shifted_t(t, n):
    y = lax.rem(lax.div(t, 4) + lax.div(n, 4), 4)
    return y * 4 + lax.rem(t + n, 4)


def wait_bytes(ref, sem):
    pltpu.make_async_copy(ref, ref, sem).wait()


def steps(parts, h):
    def over(fn):
        first = sum(parts[:h]) // STEP

        @pl.loop(first, first + parts[h] // STEP)
        def _(c):
            fn(pl.ds(pl.multiple_of(c * STEP, STEP), STEP))

    return over


def route_kernel(
    owner_block_any, block_owner_any, owner_count_any, grad,
    left_root_any, right_root_any, left_stat_any, right_stat_any,
    new_left, new_right, update,
    owner_block, block_owner, owner_count, left_root, right_root,
    inter_0, inter_1, stage_0, stage_1, held, total, mixed, done, ret_0, ret_1, back_0, back_1,
    local_sem, send_sem, recv_sem, heard_sem,
):
    f = lax.axis_index("fsdp")
    t = lax.axis_index("tp")
    me = f * TP + t
    x, core = f // 2, f % 2
    my_chunk = swapped(f)
    inter, stage = (inter_0, inter_1), (stage_0, stage_1)
    ret, back = (ret_0, ret_1), (back_0, back_1)

    fetches = [
        pltpu.make_async_copy(src, dst, local_sem.at[i])
        for i, (src, dst) in enumerate((
            (owner_block_any, owner_block),
            (block_owner_any, block_owner),
            (owner_count_any, owner_count),
            (left_root_any, left_root),
            (right_root_any, right_root),
            (left_stat_any, new_left),
            (right_stat_any, new_right),
        ))
    ]

    targets = [swapped((f * PER + q) % FS) for q in range(PER)]
    sources = [(band * FS + my_chunk) // PER for band in range(PER)]
    spread_to = [(f * PER + q) // FS * TP + t for q in range(PER)]
    barrier = pltpu.get_barrier_semaphore()

    for band in range(PER):
        for n in range(TP):
            pl.semaphore_signal(
                barrier, inc=1, device_id=(sources[band], (t + n) % TP), device_id_type=MESH
            )

    pl.semaphore_wait(barrier, PER * TP)

    def tell_targets(sem):
        for to_f in targets:
            pl.semaphore_signal(sem, inc=1, device_id=(to_f, t), device_id_type=MESH)

    tell_targets(heard_sem.at[0])

    for h in range(2):
        @pl.loop(0, TP)
        def _(n):
            to_t = shifted_t(t, lax.rem(n * 5, TP))
            for q in range(PER):
                pltpu.make_async_remote_copy(
                    src_ref=grad.at[piece(q, IN, h, to_t)],
                    dst_ref=inter[h].at[spread_to[q]],
                    send_sem=send_sem.at[0, h],
                    recv_sem=recv_sem.at[0, h],
                    device_id=(targets[q], to_t),
                    device_id_type=MESH,
                ).start()

    for fetch in fetches:
        fetch.start()

    pl.semaphore_wait(heard_sem.at[0], PER)
    tell_targets(heard_sem.at[1])
    for fetch in fetches[:3]:
        fetch.wait()

    for to_core in range(2):
        for h in range(2):
            if to_core == 0:
                wait_bytes(inter[h], recv_sem.at[0, h])
                if h == 0:
                    pl.semaphore_wait(heard_sem.at[1], PER)

            def serve(n):
                to_f = lax.rem(x + lax.div(n, TP), 4) * 2 + to_core
                to_t = shifted_t(t, lax.rem(n, TP))
                o = to_f * TP + to_t
                stage[h][o] = inter[h][owner_block[o]]
                pltpu.make_async_remote_copy(
                    src_ref=stage[h].at[o],
                    dst_ref=held.at[piece(my_chunk, IN, h, t)],
                    send_sem=send_sem.at[1, h],
                    recv_sem=recv_sem.at[1, h],
                    device_id=(to_f, to_t),
                    device_id_type=MESH,
                ).start()

            @pl.when(core == to_core)
            def _():
                stage[h][me] = inter[h][owner_block[me]]
                pltpu.make_async_copy(
                    stage[h].at[me], held.at[piece(my_chunk, IN, h, t)], recv_sem.at[1, h]
                ).start()

            @pl.when(core != to_core)
            def _():
                serve(jnp.int32(0))

            @pl.loop(1, OWNERS // 2)
            def _(n):
                serve(lax.rem(n * 53, OWNERS // 2))

    fetches[3].wait()
    fetches[4].wait()

    def mix(h):
        @steps(IN, h)
        def _(cols):
            mixed[:, cols] = jnp.dot(
                left_root[...], held[:, cols], preferred_element_type=jnp.float32
            ).astype(jnp.bfloat16)

    def finish(h, cols):
        rows = part_cols(IN, h)
        return jnp.dot(
            mixed[:, rows], right_root[rows, cols], preferred_element_type=jnp.float32
        )

    wait_bytes(held.at[:, part_cols(IN, 0)], recv_sem.at[1, 0])
    mix(0)

    @steps((BS,), 0)
    def _(cols):
        total[:, cols] = finish(0, cols)

    wait_bytes(held.at[:, part_cols(IN, 1)], recv_sem.at[1, 1])
    mix(1)

    for h in range(2):
        @steps(OUT, h)
        def _(cols):
            done[:, cols] = (total[:, cols] + finish(1, cols)).astype(jnp.bfloat16)

        pltpu.make_async_copy(
            done.at[piece(my_chunk, OUT, h, t)], ret[h].at[me], recv_sem.at[2, h]
        ).start()

        @pl.loop(1, OWNERS)
        def _(n):
            m = lax.rem(n * 69, OWNERS)
            to_f = lax.rem(x + lax.div(m, 32), 4) * 2 + lax.rem(core + lax.div(m, TP), 2)
            to_t = shifted_t(t, lax.rem(m, TP))
            pltpu.make_async_remote_copy(
                src_ref=done.at[piece(swapped(to_f), OUT, h, to_t)],
                dst_ref=ret[h].at[me],
                send_sem=send_sem.at[2, h],
                recv_sem=recv_sem.at[2, h],
                device_id=(to_f, to_t),
                device_id_type=MESH,
            ).start()

    count = owner_count[me].astype(jnp.float32)

    def add_statistics():
        for sem, stat, axis in ((6, new_right, 0), (5, new_left, 1)):
            fetches[sem].wait()

            @steps((BS,), 0)
            def _(some):
                lhs = held[:, some] if axis == 0 else held[some, :]
                stat[some, :] += count * lax.dot_general(
                    lhs, held[...], (((axis,), (axis,)), ((), ())),
                    preferred_element_type=jnp.float32,
                )

    pl.when(core == 0)(add_statistics)

    for h in range(2):
        wait_bytes(ret[h], recv_sem.at[2, h])

        @pl.loop(0, TP)
        def _(n):
            to_t = shifted_t(t, lax.rem(n * 5, TP))
            for band in range(PER):
                b = band * TP + to_t
                back[h][b] = ret[h][block_owner[b]]
                pltpu.make_async_remote_copy(
                    src_ref=back[h].at[b],
                    dst_ref=update.at[piece((band * FS + my_chunk) % PER, OUT, h, t)],
                    send_sem=send_sem.at[3, h],
                    recv_sem=recv_sem.at[3, h],
                    device_id=(sources[band], to_t),
                    device_id_type=MESH,
                ).start()

    pl.when(core == 1)(add_statistics)

    others = pl.ds(0, OWNERS - 1)
    for h in range(2):
        wait_bytes(inter[h], send_sem.at[0, h])
        wait_bytes(stage[h].at[others], send_sem.at[1, h])
        wait_bytes(ret[h].at[others], send_sem.at[2, h])
        wait_bytes(back[h], send_sem.at[3, h])
        wait_bytes(update.at[:, part_cols(OUT, h)], recv_sem.at[3, h])


def route(*operands):
    grad = operands[3]
    vmem = pl.BlockSpec(memory_space=pltpu.VMEM)
    stat = pltpu.VMEM((BS, BS), jnp.float32)
    square = pltpu.VMEM((BS, BS), jnp.bfloat16)
    return pl.pallas_call(
        route_kernel,
        out_shape=(stat, stat, pltpu.VMEM(grad.shape, jnp.bfloat16)),
        in_specs=[pl.BlockSpec(memory_space=pltpu.HBM)] * 8,
        out_specs=(vmem,) * 3,
        scratch_shapes=[
            pltpu.SMEM((OWNERS,), jnp.int32),
            pltpu.SMEM((NB,), jnp.int32),
            pltpu.SMEM((OWNERS,), jnp.int32),
            square,
            square,
            *[pltpu.VMEM((NB, RR, w // 2), jnp.bfloat16) for w in IN],
            *[pltpu.VMEM((OWNERS, RR, w // 2), jnp.bfloat16) for w in IN],
            square,
            pltpu.VMEM((BS, BS), jnp.float32),
            square,
            square,
            *[pltpu.VMEM((OWNERS, RR, w // 2), jnp.bfloat16) for w in OUT],
            *[pltpu.VMEM((NB, RR, w // 2), jnp.bfloat16) for w in OUT],
            pltpu.SemaphoreType.DMA((7,)),
            pltpu.SemaphoreType.DMA((4, 2)),
            pltpu.SemaphoreType.DMA((4, 2)),
            pltpu.SemaphoreType.REGULAR((2,)),
        ],
        compiler_params=pltpu.CompilerParams(
            collective_id=0, has_side_effects=True, vmem_limit_bytes=40 * 1024 * 1024
        ),
        cost_estimate=pl.CostEstimate(
            flops=8 * BS**3, bytes_accessed=24 * BS * BS, transcendentals=0
        ),
        name="route",
    )(*(pltpu.with_memory_space_constraint(a, pltpu.HBM) for a in operands))


def write_kernel(left, right, update, left_out, right_out, update_out, sems):
    copies = []
    for src, dst, parts in ((left, left_out, 4), (right, right_out, 4), (update, update_out, 1)):
        rows = src.shape[0] // parts
        for i in range(parts):
            piece = pl.ds(i * rows, rows)
            copies.append(pltpu.make_async_copy(src.at[piece], dst.at[piece], sems.at[len(copies)]))
    for copy in copies:
        copy.start()
    for copy in copies:
        copy.wait()


def write(*arrays):
    return pl.pallas_call(
        write_kernel,
        out_shape=tuple(jax.ShapeDtypeStruct(a.shape, a.dtype) for a in arrays),
        in_specs=[pl.BlockSpec(memory_space=pltpu.VMEM)] * 3,
        out_specs=(pl.BlockSpec(memory_space=pltpu.HBM),) * 3,
        scratch_shapes=[pltpu.SemaphoreType.DMA((9,))],
        compiler_params=pltpu.CompilerParams(vmem_limit_bytes=1024 * 1024),
        cost_estimate=pl.CostEstimate(flops=0, bytes_accessed=18 * BS * BS, transcendentals=0),
        name="write",
    )(*(pltpu.with_memory_space_constraint(a, pltpu.VMEM) for a in arrays))


def body(grad, left_stat, right_stat, left_root, right_root, block_owner, owner_block, owner_count):
    new_left, new_right, update = write(*route(
        owner_block, block_owner, owner_count, grad,
        left_root[0], right_root[0], left_stat[0], right_stat[0],
    ))
    return new_left[None], new_right[None], update


def solution(mesh):
    whole = P(("fsdp", "tp"), None, None)
    return jax.shard_map(
        body,
        mesh=mesh,
        in_specs=(P("fsdp", "tp"), whole, whole, whole, whole, P(), P(), P()),
        out_specs=(whole, whole, P("fsdp", "tp")),
        check_vma=False,
    )
```
